256 devices in a mesh: blk: 16 (over y, x), exc: 8 (over z), row: 2 (over core).
Axes of the slice: x: 4, y: 4, z: 8, core: 2. Of those that a mesh axis runs over, the one named last changes fastest.
Arguments:
- panels: bfloat16 [128, 3072, 128], P('blk', 'row'), may hold values from -6 to 6
- patterns: bfloat16 [128, 128, 256], P('blk', 'row'), may hold values from -6 to 6
- geometry: bfloat16 [32, 3072, 256], P('blk', 'row'), may hold values from -0.109375 to 0.109375
- excitations: bfloat16 [32, 768, 3072], P('blk', 'exc', 'row'), may hold values from -0.109375 to 0.109375
- moved_blocks: int32 [32], replicated, may hold values from 0 to 127, as said below
- partners: int32 [32, 2048], P(None, ('blk', 'exc')), may hold values from 0 to 127, as said below
- translation: float32 [32, 2048, 256], P(None, ('blk', 'exc')), may hold values from -0.375 to 0.375
Outputs:
- couplings: bfloat16 [32, 2048, 128, 128], P(None, ('blk', 'exc'), 'row')
- projections: float32 [32, 768, 128], P('blk', 'exc')
The draws below stay inside these ranges and needn't reach their ends.
Inputs may be any that keep to these rules, and one draw needn't show every extreme that they name: `moved_blocks`: distinct blocks; at most 3 of them lie among the 8 consecutive blocks of any one group, and exactly 3 in some group. `partners`: the block in column j lies in the group of 8 consecutive blocks numbered j * 128 // 16384.
All inputs are finite; a program needn't handle non-finite values.
Results may differ from the reference program's by a relative error of at most 0.0058.
Values may be sent and summed in bfloat16 or wider, within the bound.
No kernel may reach another device: no remote copies, remote signals or barrier semaphores. Data moves between devices by JAX's collectives and lax.ppermute only.
A program may use at most 128 MiB of HBM per device.

```python
import jax
import jax.numpy as jnp
from jax import lax

K = 128
P_SIZE = 256
CAP = 3
BLK_DEV = 8
NB = 128
R = 3072
M = 32
NE = 768
NP = 2048


def draw_moved_blocks(key, part):
    key = jax.random.fold_in(key, 11)
    key_hot, key_others, key_slots, key_order = jax.random.split(key, 4)
    owners = NB // BLK_DEV
    hottest = jax.random.randint(key_hot, (), 0, owners)
    others = jax.random.permutation(key_others, owners - 1)
    others = others + (others >= hottest).astype(jnp.int32)
    position = jnp.arange(M)
    extra_slot = jnp.maximum(position - CAP, 0)
    owner_of = jnp.where(position < CAP, hottest, others[extra_slot % (owners - 1)])
    rank_within = jnp.where(position < CAP, position, extra_slot // (owners - 1))
    shuffled = jax.vmap(lambda sub: jax.random.permutation(sub, BLK_DEV))(jax.random.split(key_slots, owners))
    local_slot = shuffled[owner_of, rank_within]
    chosen = owner_of * BLK_DEV + local_slot
    reorder = jax.random.permutation(key_order, M)
    return chosen[reorder].astype(jnp.int32)


def draw_partners(key, part):
    key = jax.random.fold_in(key, 23)
    column = jnp.arange(NP)
    group_index = column * NB // (NP * BLK_DEV)
    local_slot = jax.random.randint(key, (M, NP), 0, BLK_DEV)
    return (group_index[None, :] * BLK_DEV + local_slot).astype(jnp.int32)


def block_levels(key, dims, cuts, low, top_value):
    level = 1.0
    for dim, shards_of in cuts:
        draws = jax.random.uniform(jax.random.fold_in(jax.random.fold_in(key, 6), dim), (shards_of,), jnp.float32, low / len(cuts), top_value / len(cuts))
        level = level * jnp.repeat(jnp.exp(draws), dims[dim] // shards_of).reshape((-1,) + (1,) * (len(dims) - 1 - dim))
    return level


def normal_values(own_key, extent, width, limit, cuts=(), kind=jnp.bfloat16):
    factor_of = block_levels(own_key, extent, cuts, -0.22, 0.18) if cuts else 1.0
    result = jax.random.normal(own_key, extent, jnp.float32) * width * factor_of
    return jnp.minimum(jnp.maximum(result, -limit), limit).astype(kind)


def setup_inputs(seed: int = 0) -> dict:
    key_list = jax.random.split(jax.random.key(seed), 8)
    return {
        "panels": normal_values(key_list[0], (NB, R, K), 1.0, 6.0, ((0, 16), (1, 2))),
        "patterns": normal_values(key_list[1], (NB, K, P_SIZE), 1.0, 6.0, ((0, 16), (1, 2))),
        "geometry": normal_values(key_list[2], (M, R, P_SIZE), R ** -0.5, 0.109375, ((0, 16), (1, 2))),
        "excitations": normal_values(key_list[3], (M, NE, R), R ** -0.5, 0.109375, ((0, 16), (1, 8), (2, 2))),
        "moved_blocks": draw_moved_blocks(jax.random.fold_in(key_list[7], 71), 0),
        "partners": draw_partners(jax.random.fold_in(key_list[7], 71), 0),
        "translation": normal_values(key_list[6], (M, NP, P_SIZE), P_SIZE ** -0.5, 0.375, ((1, 128),), jnp.float32),
    }


def reference(panels, patterns, geometry, excitations, moved_blocks, partners, translation):
    moved_panels = panels[moved_blocks].astype(jnp.float32)
    radiation = jnp.einsum("mrl,mrp->mlp", moved_panels, geometry.astype(jnp.float32), precision=lax.Precision.HIGHEST).astype(jnp.bfloat16)
    projections = jnp.einsum("mer,mrl->mel", excitations.astype(jnp.float32), moved_panels, precision=lax.Precision.HIGHEST)

    def one_block(inputs_one):
        partner_ids, factor, pattern_row = inputs_one
        chosen = patterns[partner_ids].astype(jnp.float32)
        weighted = (chosen * factor[:, None, :]).astype(jnp.bfloat16)
        return jnp.einsum("jkp,lp->jkl", weighted.astype(jnp.float32), pattern_row.astype(jnp.float32), precision=lax.Precision.HIGHEST).astype(jnp.bfloat16)

    couplings = lax.map(one_block, (partners, translation, radiation))
    return couplings, projections
```

```python
import jax
import jax.numpy as jnp
from jax import lax
from jax.experimental import pallas as pl
from jax.experimental.pallas import tpu as pltpu
from jax.sharding import PartitionSpec as P

CAP = 3
SIDE = 4
DEPTH = 8
MOVED = 32
AXES = ("blk", "exc", "row")
NT = (((1,), (1,)), ((), ()))
SMEM = pl.BlockSpec(memory_space=pltpu.SMEM)
VMEM = pl.BlockSpec(memory_space=pltpu.VMEM)


def device_id(y, x, z, core):
    return ((y * SIDE + x) * DEPTH + z) * 2 + core


def plane_perm(shift, first):
    pairs = []
    for y in range(SIDE):
        for x in range(SIDE):
            for z in range(DEPTH):
                for core in range(2):
                    along_x = (core == 0) == first
                    y_to = y if along_x else (y + shift) % SIDE
                    x_to = (x + shift) % SIDE if along_x else x
                    pairs.append((device_id(y, x, z, core), device_id(y_to, x_to, z, core)))
    return pairs


def depth_perm(shift):
    pairs = []
    for y in range(SIDE):
        for x in range(SIDE):
            for z in range(DEPTH):
                for core in range(2):
                    z_to = (z + (shift if core == 0 else -shift)) % DEPTH
                    pairs.append((device_id(y, x, z, core), device_id(y, x, z_to, core)))
    return pairs


def plane_send(value, first):
    return [lax.ppermute(value, AXES, plane_perm(s, first)) for s in range(1, SIDE)]


def core_swap(value):
    return lax.ppermute(value, "row", [(0, 1), (1, 0)])


def pick_kernel(moved, panels, out, slots, buf, sem):
    me = lax.axis_index("blk")
    z = lax.axis_index("exc")
    for s in range(CAP):
        slots[s] = 0
    count = jnp.int32(0)
    for i in range(MOVED):
        block = moved[i]
        mine = (block >> 3) == me

        @pl.when(mine)
        def _():
            slots[count] = block & 7

        count = count + mine.astype(jnp.int32)
    copies = []
    for s in range(CAP):
        copy = pltpu.make_async_copy(panels.at[slots[s]], buf.at[s], sem.at[s])
        copy.start()
        copies.append(copy)
    width = buf.shape[2]
    share = out.shape[1]
    rows = lax.broadcasted_iota(jnp.int32, (share, width), 0)
    cols = lax.broadcasted_iota(jnp.int32, (share, width), 1)
    chosen = jnp.where(cols == rows + z * share, 1.0, 0.0).astype(jnp.bfloat16)
    for s in range(CAP):
        copies[s].wait()
        out[s] = lax.dot_general(chosen, buf[s], NT, preferred_element_type=jnp.float32).astype(jnp.bfloat16)


def pick(moved_blocks, panels):
    blocks, rows, width = panels.shape
    share = width // DEPTH
    return pl.pallas_call(
        pick_kernel,
        out_shape=jax.ShapeDtypeStruct((CAP, share, rows), jnp.bfloat16),
        in_specs=[SMEM, pl.BlockSpec(memory_space=pl.ANY)],
        out_specs=VMEM,
        scratch_shapes=[
            pltpu.SMEM((CAP,), jnp.int32),
            pltpu.VMEM((CAP, rows, width), jnp.bfloat16),
            pltpu.SemaphoreType.DMA((CAP,)),
        ],
        name="pick",
    )(moved_blocks, panels)


def route_kernel(moved, a0, a1, a2, a3, o0, o1, o2, o3, count, rank):
    me = lax.axis_index("blk")
    core = lax.axis_index("row")
    y, x = me >> 2, me & 3
    on_x = core == 0
    here = jnp.where(on_x, x, y)
    across = jnp.where(on_x, y, x)
    for g in range(SIDE * SIDE):
        count[g] = 0
    for i in range(MOVED):
        owner = moved[i] >> 3
        seen = count[owner]
        rank[i] = seen
        count[owner] = seen + 1
    arrivals = (a0, a1, a2, a3)
    for t, out in enumerate((o0, o1, o2, o3)):
        target = (across + t) & 3
        block = jnp.where(on_x, target * SIDE + here, here * SIDE + target)
        for s in range(2):
            index = 2 * block + s
            owner = moved[index] >> 3
            slot = rank[index]
            owner_y, owner_x = owner >> 2, owner & 3
            found = jnp.where(on_x, owner_y, owner_x) == across
            source = (here - jnp.where(on_x, owner_x, owner_y)) & 3
            out[s] = jnp.zeros_like(out[s])
            for k in range(SIDE):

                @pl.when(found & (source == k))
                def _(k=k, s=s, out=out, slot=slot):
                    out[s] = arrivals[k][slot]


def route(moved_blocks, arrivals):
    _, share, rows = arrivals[0].shape
    return pl.pallas_call(
        route_kernel,
        out_shape=[jax.ShapeDtypeStruct((2, share, rows), jnp.bfloat16)] * SIDE,
        in_specs=[SMEM] + [VMEM] * SIDE,
        out_specs=[VMEM] * SIDE,
        scratch_shapes=[pltpu.SMEM((SIDE * SIDE,), jnp.int32), pltpu.SMEM((MOVED,), jnp.int32)],
        name="route",
    )(moved_blocks, *arrivals)


def radiate_kernel(a0, a1, a2, a3, geometry, columns, partial):
    rows = a0.shape[2]
    for s in range(2):
        panel = (a0[s] + a1[s]) + (a2[s] + a3[s])
        columns[s, :, :rows] = panel
        columns[s, :, rows:] = jnp.zeros((panel.shape[0], columns.shape[2] - rows), jnp.bfloat16)
        partial[s] = jnp.dot(panel, geometry[s], preferred_element_type=jnp.float32)


def radiate(arrivals, geometry):
    _, share, rows = arrivals[0].shape
    return pl.pallas_call(
        radiate_kernel,
        out_shape=[
            jax.ShapeDtypeStruct((2, share, rows + rows // 3), jnp.bfloat16),
            jax.ShapeDtypeStruct((2, share, geometry.shape[2]), jnp.float32),
        ],
        in_specs=[VMEM] * 5,
        out_specs=[VMEM] * 2,
        name="radiate",
    )(*arrivals, geometry)


def assemble_kernel(own, r1, r2, r3, w1, w2, w3, far, out):
    z = lax.axis_index("exc")
    core = lax.axis_index("row")
    sign = 1 - 2 * core
    share = own.shape[1]

    def place(source, value):
        start = pl.multiple_of((source & 7) * share, share)
        out[pl.ds(start, share), :] = value

    place(z, own[core])
    for k, (r, w) in enumerate(((r1, w1), (r2, w2), (r3, w3)), start=1):
        place(z - sign * k + DEPTH, r[core])
        place(z + sign * k + DEPTH, w[core])
    place(z + 4, far[...])


def assemble(own, direct, swapped, far):
    _, share, width = own.shape
    return pl.pallas_call(
        assemble_kernel,
        out_shape=jax.ShapeDtypeStruct((DEPTH * share, width), jnp.bfloat16),
        in_specs=[VMEM] * 8,
        out_specs=VMEM,
        name="assemble",
    )(own, *direct, *swapped, far)


def couple(ids, slots, pieces, translation, patterns, so_far=None):
    n = len(pieces)
    moved, columns, width = translation.shape
    _, rows, _ = patterns.shape
    basis = pieces[0].shape[1]
    together = 4

    def kernel(ids_ref, slots_ref, *refs):
        piece_refs = refs[:n]
        trans, patt = refs[n], refs[n + 1]
        out = refs[-1]
        step = pl.program_id(0)
        moved_id = ids_ref[step]
        rad = piece_refs[0][0]
        for p in range(1, n):
            rad = jnp.where(step >= 4 * p, piece_refs[p][0], rad)
        for first in range(0, columns, together):
            parts = []
            for j in range(first, first + together):
                pattern = patt[slots_ref[moved_id, j]].astype(jnp.float32)
                parts.append((pattern * trans[0, j : j + 1, :]).astype(jnp.bfloat16))
            weighted = jnp.concatenate(parts, axis=0)
            block = lax.dot_general(weighted, rad, NT, preferred_element_type=jnp.float32)
            out[0, first : first + together] = block.astype(jnp.bfloat16).reshape(together, rows, basis)

    def piece_spec(p):
        return pl.BlockSpec((1, basis, width), lambda g, ids_ref, slots_ref: (jnp.clip(g - 4 * p, 0, 3), 0, 0))

    in_specs = [piece_spec(p) for p in range(n)]
    in_specs.append(pl.BlockSpec((1, columns, width), lambda g, ids_ref, slots_ref: (ids_ref[g], 0, 0)))
    in_specs.append(pl.BlockSpec(patterns.shape, lambda g, ids_ref, slots_ref: (0, 0, 0)))
    operands = [*pieces, translation, patterns]
    aliases = {}
    if so_far is not None:
        in_specs.append(pl.BlockSpec(memory_space=pl.ANY))
        aliases = {2 + len(operands): 0}
        operands.append(so_far)
    return pl.pallas_call(
        kernel,
        out_shape=jax.ShapeDtypeStruct((moved, columns, rows, basis), jnp.bfloat16),
        grid_spec=pltpu.PrefetchScalarGridSpec(
            num_scalar_prefetch=2,
            grid=(4 * n,),
            in_specs=in_specs,
            out_specs=pl.BlockSpec((1, columns, rows, basis), lambda g, ids_ref, slots_ref: (ids_ref[g], 0, 0, 0)),
        ),
        input_output_aliases=aliases,
        cost_estimate=pl.CostEstimate(
            flops=4 * n * columns * rows * width * basis * 4,
            bytes_accessed=4 * n * columns * rows * basis * 2,
            transcendentals=0,
        ),
        name="couple",
    )(ids, slots, *operands)


def project_kernel(excitations, gathered, out):
    rows = excitations.shape[2]
    for s in range(2):
        panel = gathered[:, s, :, :rows].reshape(-1, rows)
        out[s] = lax.dot_general(excitations[s], panel, NT, preferred_element_type=jnp.float32)


def project(excitations, gathered):
    moved, count, _ = excitations.shape
    basis = gathered.shape[0] * gathered.shape[2]
    return pl.pallas_call(
        project_kernel,
        out_shape=jax.ShapeDtypeStruct((moved, count, basis), jnp.float32),
        in_specs=[VMEM] * 2,
        out_specs=VMEM,
        name="project",
    )(excitations, gathered)


def piece_ids(y, x, core, leg):
    k = jnp.arange(SIDE)
    near = jnp.where(core == 0, x, y)
    far = jnp.where(core == 0, y, x)
    first = (near - k) & 3
    second = (far - leg) & 3
    block = jnp.where(core == 0, second * SIDE + first, first * SIDE + second)
    return 2 * block + core


def on_device(panels, patterns, geometry, excitations, moved_blocks, partners, translation):
    me = lax.axis_index("blk")
    core = lax.axis_index("row")
    y, x = me >> 2, me & 3
    slots = partners & 7

    outgoing = pick(moved_blocks, panels)
    routed = route(moved_blocks, [outgoing, *plane_send(outgoing, True)])
    landed = [lax.ppermute(routed[s], AXES, plane_perm(s, False)) for s in range(1, SIDE)]
    columns, partial = radiate([routed[0], *landed], geometry)
    gathered = lax.all_gather(columns, "exc", axis=0)

    radiation = (partial + core_swap(partial)).astype(jnp.bfloat16)
    half = lax.dynamic_index_in_dim(radiation, core, 0, keepdims=False)
    direct = [lax.ppermute(radiation, AXES, depth_perm(k)) for k in range(1, 4)]
    far = lax.ppermute(half, AXES, depth_perm(4))
    swapped = [core_swap(value) for value in direct]
    mine = assemble(radiation, direct, swapped, far)

    stack = jnp.stack([mine, *plane_send(mine, True)])
    arrived = plane_send(stack, False)
    stack_other = core_swap(stack)
    arrived_other = [core_swap(value) for value in arrived]
    other = 1 - core
    ids_near = jnp.concatenate([piece_ids(y, x, core, 0), piece_ids(y, x, other, 0)])
    ids_own = jnp.concatenate([piece_ids(y, x, core, leg) for leg in range(1, 4)])
    ids_other = jnp.concatenate([piece_ids(y, x, other, leg) for leg in range(1, 4)])
    couplings = couple(ids_near, slots, [stack, stack_other], translation, patterns)
    couplings = couple(ids_own, slots, arrived, translation, patterns, couplings)
    couplings = couple(ids_other, slots, arrived_other, translation, patterns, couplings)

    projected = project(excitations, gathered)
    projected = projected + core_swap(projected)
    return (couplings, projected)


def solution(mesh):
    placed = (
        P("blk", "row", None),
        P("blk", "row", None),
        P("blk", "row", None),
        P("blk", "exc", "row"),
        P(),
        P(None, ("blk", "exc")),
        P(None, ("blk", "exc"), None),
    )
    return jax.shard_map(
        on_device,
        mesh=mesh,
        in_specs=placed,
        out_specs=(P(None, ("blk", "exc"), "row", None), P("blk", "exc", None)),
        check_vma=False,
    )
```

```python
import jax
import jax.numpy as jnp
from jax import lax
from jax.experimental import pallas as pl
from jax.experimental.pallas import tpu as pltpu
from jax.sharding import PartitionSpec as P

CAP = 3
SIDE = 4
DEPTH = 8
MOVED = 32
SLICES = 4
ORDER = (1, 3, 2)
MIB = 2**20
AXES = ("blk", "exc", "row")
NT = (((1,), (1,)), ((), ()))
SMEM = pl.BlockSpec(memory_space=pltpu.SMEM)
VMEM = pl.BlockSpec(memory_space=pltpu.VMEM)


def device_id(y, x, z, core):
    return ((y * SIDE + x) * DEPTH + z) * 2 + core


def plane_perm(shift, first):
    pairs = []
    for y in range(SIDE):
        for x in range(SIDE):
            for z in range(DEPTH):
                for core in range(2):
                    along_x = (core == 0) == first
                    y_to = y if along_x else (y + shift) % SIDE
                    x_to = (x + shift) % SIDE if along_x else x
                    pairs.append((device_id(y, x, z, core), device_id(y_to, x_to, z, core)))
    return pairs


def depth_perm(shift):
    pairs = []
    for y in range(SIDE):
        for x in range(SIDE):
            for z in range(DEPTH):
                for core in range(2):
                    pairs.append((device_id(y, x, z, core), device_id(y, x, (z + shift) % DEPTH, core)))
    return pairs


def plane_send(value, first):
    sent = {s: lax.ppermute(value, AXES, plane_perm(s, first)) for s in ORDER}
    return [sent[s] for s in range(1, SIDE)]


def depth_send(value):
    return [lax.ppermute(value, AXES, depth_perm(s)) for s in (1, -1, 2)]


def core_swap(value):
    return lax.ppermute(value, "row", [(0, 1), (1, 0)])


def limit(mib):
    return pltpu.CompilerParams(vmem_limit_bytes=mib * MIB)


def pick_kernel(moved, panels, *refs):
    staged = (len(refs) - 4) // 2
    sources, out, copies_to = refs[:staged], refs[staged], refs[staged + 1 : 2 * staged + 1]
    buf, sem, stage_sem = refs[-3:]
    me = lax.axis_index("blk")
    part = lax.axis_index("exc") & (SLICES - 1)
    slots = [jnp.int32(0)] * CAP
    count = jnp.int32(0)
    for i in range(MOVED):
        block = moved[i]
        mine = (block >> 3) == me
        slots = [jnp.where(mine & (count == s), block & 7, slots[s]) for s in range(CAP)]
        count = count + mine.astype(jnp.int32)
    copies = []
    for s in range(CAP):
        copy = pltpu.make_async_copy(panels.at[slots[s]], buf.at[s], sem.at[s])
        copy.start()
        copies.append(copy)
    stages = []
    for n in range(staged):
        copy = pltpu.make_async_copy(sources[n], copies_to[n], stage_sem.at[n])
        copy.start()
        stages.append(copy)
    width = buf.shape[2]
    share = out.shape[1]
    rows = lax.broadcasted_iota(jnp.int32, (share, width), 0)
    cols = lax.broadcasted_iota(jnp.int32, (share, width), 1)
    chosen = jnp.where(cols == rows + part * share, 1.0, 0.0).astype(jnp.bfloat16)
    for s in range(CAP):
        copies[s].wait()
        out[s] = lax.dot_general(chosen, buf[s], NT, preferred_element_type=jnp.float32).astype(jnp.bfloat16)
    for copy in stages:
        copy.wait()


def pick(moved_blocks, panels, *others):
    blocks, rows, width = panels.shape
    share = width // SLICES
    n = len(others)
    in_hbm = [pltpu.with_memory_space_constraint(value, pltpu.HBM) for value in (panels, *others)]
    picked = jax.ShapeDtypeStruct((CAP, share, rows), jnp.bfloat16)
    return pl.pallas_call(
        pick_kernel,
        out_shape=[picked] + [jax.ShapeDtypeStruct(value.shape, value.dtype) for value in others],
        in_specs=[SMEM] + [pl.BlockSpec(memory_space=pltpu.HBM)] * (1 + n),
        out_specs=[VMEM] * (1 + n),
        scratch_shapes=[
            pltpu.VMEM((CAP, rows, width), jnp.bfloat16),
            pltpu.SemaphoreType.DMA((CAP,)),
            pltpu.SemaphoreType.DMA((n,)),
        ],
        compiler_params=limit(12),
        name="pick",
    )(moved_blocks, *in_hbm)


def route_kernel(moved, a0, a1, a2, a3, o0, o1, o2, o3, count, rank):
    me = lax.axis_index("blk")
    core = lax.axis_index("row")
    y, x = me >> 2, me & 3
    on_x = core == 0
    here = jnp.where(on_x, x, y)
    across = jnp.where(on_x, y, x)
    for g in range(SIDE * SIDE):
        count[g] = 0
    for i in range(MOVED):
        owner = moved[i] >> 3
        seen = count[owner]
        rank[i] = seen
        count[owner] = seen + 1
    arrivals = (a0, a1, a2, a3)
    for t, out in enumerate((o0, o1, o2, o3)):
        target = (across + t) & 3
        block = jnp.where(on_x, target * SIDE + here, here * SIDE + target)
        for s in range(2):
            index = 2 * block + s
            owner = moved[index] >> 3
            slot = rank[index]
            owner_y, owner_x = owner >> 2, owner & 3
            found = jnp.where(on_x, owner_y, owner_x) == across
            source = (here - jnp.where(on_x, owner_x, owner_y)) & 3
            value = jnp.zeros(out.shape[1:], out.dtype)
            for k in range(SIDE):
                value = jnp.where(found & (source == k), arrivals[k][slot], value)
            out[s] = value


def route(moved_blocks, arrivals):
    _, share, rows = arrivals[0].shape
    return pl.pallas_call(
        route_kernel,
        out_shape=[jax.ShapeDtypeStruct((2, share, rows), jnp.bfloat16)] * SIDE,
        in_specs=[SMEM] + [VMEM] * SIDE,
        out_specs=[VMEM] * SIDE,
        scratch_shapes=[pltpu.SMEM((SIDE * SIDE,), jnp.int32), pltpu.SMEM((MOVED,), jnp.int32)],
        compiler_params=limit(6),
        name="route",
    )(moved_blocks, *arrivals)


def radiate_kernel(a0, a1, a2, a3, geometry, columns, keep, give):
    core = lax.axis_index("row")
    partial = []
    for s in range(2):
        panel = (a0[s] + a1[s]) + (a2[s] + a3[s])
        columns[s] = panel
        partial.append(jnp.dot(panel, geometry[s], preferred_element_type=jnp.float32))
    keep[...] = jnp.where(core == 0, partial[0], partial[1])
    give[...] = jnp.where(core == 0, partial[1], partial[0])


def radiate(arrivals, geometry):
    _, share, rows = arrivals[0].shape
    half = jax.ShapeDtypeStruct((share, geometry.shape[2]), jnp.float32)
    return pl.pallas_call(
        radiate_kernel,
        out_shape=[jax.ShapeDtypeStruct((2, share, rows), jnp.bfloat16), half, half],
        in_specs=[VMEM] * 5,
        out_specs=[VMEM] * 3,
        compiler_params=limit(8),
        name="radiate",
    )(*arrivals, geometry)


def assemble_kernel(own, up, down, far, out):
    z = lax.axis_index("exc")
    share = own.shape[0]
    for shift, value in ((0, own), (1, up), (-1, down), (2, far)):
        start = pl.multiple_of(((z - shift) & (SLICES - 1)) * share, share)
        out[pl.ds(start, share), :] = value[...]


def assemble(pieces):
    share, width = pieces[0].shape
    return pl.pallas_call(
        assemble_kernel,
        out_shape=jax.ShapeDtypeStruct((SLICES * share, width), jnp.bfloat16),
        in_specs=[VMEM] * 4,
        out_specs=VMEM,
        compiler_params=limit(4),
        name="assemble",
    )(*pieces)


def couple(pieces, partners, translation, patterns, so_far=None):
    n = len(pieces)
    moved, columns, width = translation.shape
    _, rows, _ = patterns.shape
    basis = pieces[0][2].shape[1]
    together = 4

    def kernel(partners_ref, trans, patt, *refs):
        piece_refs = refs[:n]
        out, buf, sem = refs[-3:]
        me = lax.axis_index("blk")
        core = lax.axis_index("row")
        y, x = me >> 2, me & 3
        copies = []
        for p, (leg, own, _) in enumerate(pieces):
            holder = core if own else 1 - core
            near = jnp.where(holder == 0, x, y)
            across = (jnp.where(holder == 0, y, x) - leg) & 3
            ids = []
            for k in range(SIDE):
                first = (near - k) & 3
                block = jnp.where(holder == 0, across * SIDE + first, first * SIDE + across)
                ids.append(2 * block + holder)
            rads = [piece_refs[p][k].T for k in range(SIDE)]
            for first in range(0, columns, together):
                for k in range(SIDE):
                    parts = []
                    for j in range(first, first + together):
                        pattern = patt[partners_ref[j, ids[k]] & 7].astype(jnp.float32)
                        parts.append((pattern * trans[ids[k], j : j + 1, :]).astype(jnp.bfloat16))
                    weighted = jnp.concatenate(parts, axis=0)
                    block = jnp.dot(weighted, rads[k], preferred_element_type=jnp.float32)
                    buf[p, k, first : first + together] = block.astype(jnp.bfloat16).reshape(together, rows, basis)
            for k in range(SIDE):
                copy = pltpu.make_async_copy(buf.at[p, k], out.at[ids[k]], sem.at[p, k])
                copy.start()
                copies.append(copy)
        for copy in copies:
            copy.wait()

    operands = [partners, translation, patterns, *[piece[2] for piece in pieces]]
    in_specs = [SMEM] + [VMEM] * (2 + n)
    aliases = {}
    if so_far is not None:
        in_specs.append(pl.BlockSpec(memory_space=pl.ANY))
        aliases = {len(operands): 0}
        operands.append(so_far)
    return pl.pallas_call(
        kernel,
        out_shape=jax.ShapeDtypeStruct((moved, columns, rows, basis), jnp.bfloat16),
        in_specs=in_specs,
        out_specs=pl.BlockSpec(memory_space=pl.ANY),
        scratch_shapes=[
            pltpu.VMEM((n, SIDE, columns, rows, basis), jnp.bfloat16),
            pltpu.SemaphoreType.DMA((n, SIDE)),
        ],
        input_output_aliases=aliases,
        compiler_params=limit(14),
        cost_estimate=pl.CostEstimate(
            flops=2 * n * SIDE * columns * rows * width * basis,
            bytes_accessed=n * SIDE * columns * rows * basis * 2,
            transcendentals=0,
        ),
        name="couple",
    )(*operands)


def project_kernel(excitations, own, up, down, far, out, panel):
    z = lax.axis_index("exc")
    share = own.shape[1]
    for shift, value in ((0, own), (1, up), (-1, down), (2, far)):
        start = pl.multiple_of(((z - shift) & (SLICES - 1)) * share, share)
        panel[:, pl.ds(start, share), :] = value[...]
    for s in range(2):
        out[s] = lax.dot_general(excitations[s], panel[s], NT, preferred_element_type=jnp.float32)


def project(excitations, pieces):
    moved, count, rows = excitations.shape
    basis = SLICES * pieces[0].shape[1]
    return pl.pallas_call(
        project_kernel,
        out_shape=jax.ShapeDtypeStruct((moved, count, basis), jnp.float32),
        in_specs=[VMEM] * 5,
        out_specs=VMEM,
        scratch_shapes=[pltpu.VMEM((2, basis, rows), jnp.bfloat16)],
        compiler_params=limit(6),
        name="project",
    )(excitations, *pieces)


def on_device(panels, patterns, geometry, excitations, moved_blocks, partners, translation):
    outgoing, geometry, translation, patterns, excitations, partners = pick(
        moved_blocks, panels, geometry, translation, patterns, excitations, partners.T
    )
    routed = route(moved_blocks, [outgoing, *plane_send(outgoing, True)])
    landed = {s: lax.ppermute(routed[s], AXES, plane_perm(s, False)) for s in ORDER}
    columns, keep, give = radiate([routed[0], *[landed[s] for s in range(1, SIDE)]], geometry)
    radiation = (keep + core_swap(give)).astype(jnp.bfloat16)
    columns, radiation = lax.optimization_barrier((columns, radiation))
    mine = assemble([radiation, *depth_send(radiation)])
    pieces = [columns, *depth_send(columns)]
    stack = jnp.stack([mine, *plane_send(mine, True)])
    arrived = plane_send(stack, False)
    couplings = couple([(0, True, stack)], partners, translation, patterns)
    couplings, *arrived = lax.optimization_barrier((couplings, *arrived))
    stack_other = core_swap(stack)
    arrived_other = [core_swap(value) for value in arrived]
    own = [(leg, True, arrived[leg - 1]) for leg in range(1, SIDE)]
    other = [(leg, False, arrived_other[leg - 1]) for leg in range(1, SIDE)]
    couplings = couple(own, partners, translation, patterns, couplings)
    couplings, *pieces = lax.optimization_barrier((couplings, *pieces))
    projected = project(excitations, pieces)
    couplings = couple([(0, False, stack_other), *other], partners, translation, patterns, couplings)
    projected = projected + core_swap(projected)
    return (couplings, projected)


def solution(mesh):
    placed = (
        P("blk", "row", None),
        P("blk", "row", None),
        P("blk", "row", None),
        P("blk", "exc", "row"),
        P(),
        P(None, ("blk", "exc")),
        P(None, ("blk", "exc"), None),
    )
    return jax.shard_map(
        on_device,
        mesh=mesh,
        in_specs=placed,
        out_specs=(P(None, ("blk", "exc"), "row", None), P("blk", "exc", None)),
        check_vma=False,
    )
```

```python
import jax
import jax.numpy as jnp
from jax import lax
from jax.experimental import pallas as pl
from jax.experimental.pallas import tpu as pltpu
from jax.sharding import PartitionSpec as P

CAP = 3
SIDE = 4
DEPTH = 8
MOVED = 32
SLICES = 4
ORDER = (1, 3, 2)
MIB = 2**20
AXES = ("blk", "exc", "row")
NT = (((1,), (1,)), ((), ()))
SMEM = pl.BlockSpec(memory_space=pltpu.SMEM)
VMEM = pl.BlockSpec(memory_space=pltpu.VMEM)
HBM = pl.BlockSpec(memory_space=pltpu.HBM)


def device_id(y, x, z, core):
    return ((y * SIDE + x) * DEPTH + z) * 2 + core


def plane_perm(shift, first):
    pairs = []
    for y in range(SIDE):
        for x in range(SIDE):
            for z in range(DEPTH):
                for core in range(2):
                    along_x = (core == 0) == first
                    y_to = y if along_x else (y + shift) % SIDE
                    x_to = (x + shift) % SIDE if along_x else x
                    pairs.append((device_id(y, x, z, core), device_id(y_to, x_to, z, core)))
    return pairs


def depth_perm(shift):
    pairs = []
    for y in range(SIDE):
        for x in range(SIDE):
            for z in range(DEPTH):
                for core in range(2):
                    step = -shift if core and shift == 2 else shift
                    pairs.append((device_id(y, x, z, core), device_id(y, x, (z + step) % DEPTH, core)))
    return pairs


def plane_send(value, first):
    sent = {s: lax.ppermute(value, AXES, plane_perm(s, first)) for s in ORDER}
    return [sent[s] for s in range(1, SIDE)]


def depth_send(value, shift):
    return lax.ppermute(value, AXES, depth_perm(shift))


def core_swap(value):
    return lax.ppermute(value, "row", [(0, 1), (1, 0)])


def limit(mib):
    return pltpu.CompilerParams(vmem_limit_bytes=mib * MIB)


def pick_kernel(moved_hbm, panels, out, moved, buf, sem):
    index_copy = pltpu.make_async_copy(moved_hbm, moved, sem.at[CAP])
    index_copy.start()
    me = lax.axis_index("blk")
    part = lax.axis_index("exc") & (SLICES - 1)
    slots = [jnp.int32(0)] * CAP
    count = jnp.int32(0)
    index_copy.wait()
    for i in range(MOVED):
        block = moved[i]
        mine = (block >> 3) == me
        slots = [jnp.where(mine & (count == s), block & 7, slots[s]) for s in range(CAP)]
        count = count + mine.astype(jnp.int32)
    copies = []
    for s in range(CAP):
        copy = pltpu.make_async_copy(panels.at[slots[s]], buf.at[s], sem.at[s])
        copy.start()
        copies.append(copy)
    width = buf.shape[2]
    share = out.shape[1]
    rows = lax.broadcasted_iota(jnp.int32, (share, width), 0)
    cols = lax.broadcasted_iota(jnp.int32, (share, width), 1)
    chosen = jnp.where(cols == rows + part * share, 1.0, 0.0).astype(jnp.bfloat16)
    for s in range(CAP):
        copies[s].wait()
        out[s] = lax.dot_general(chosen, buf[s], NT, preferred_element_type=jnp.float32).astype(jnp.bfloat16)


def in_hbm(value):
    return pltpu.with_memory_space_constraint(value, pltpu.HBM)


def pick(moved_blocks, panels):
    blocks, rows, width = panels.shape
    return pl.pallas_call(
        pick_kernel,
        out_shape=jax.ShapeDtypeStruct((CAP, width // SLICES, rows), jnp.bfloat16),
        in_specs=[HBM] * 2,
        out_specs=VMEM,
        scratch_shapes=[
            pltpu.SMEM((MOVED,), jnp.int32),
            pltpu.VMEM((CAP, rows, width), jnp.bfloat16),
            pltpu.SemaphoreType.DMA((CAP + 1,)),
        ],
        compiler_params=limit(6),
        name="pick",
    )(in_hbm(moved_blocks), in_hbm(panels))


def stage_kernel(after, moved_hbm, *refs):
    n = (len(refs) - 5) // 2
    table = refs[n]
    moved, count, rank, sem = refs[-4:]
    copies = [pltpu.make_async_copy(refs[k], refs[n + 1 + k], sem.at[k]) for k in range(n)]
    index_copy = pltpu.make_async_copy(moved_hbm, moved, sem.at[n])
    index_copy.start()
    for copy in copies:
        copy.start()
    me = lax.axis_index("blk")
    core = lax.axis_index("row")
    y, x = me >> 2, me & 3
    on_x = core == 0
    here = jnp.where(on_x, x, y)
    across = jnp.where(on_x, y, x)
    for g in range(SIDE * SIDE):
        count[g] = 0
    index_copy.wait()
    for i in range(MOVED):
        owner = moved[i] >> 3
        seen = count[owner]
        rank[i] = seen
        count[owner] = seen + 1
    for t in range(SIDE):
        target = (across + t) & 3
        block = jnp.where(on_x, target * SIDE + here, here * SIDE + target)
        for s in range(2):
            index = 2 * block + s
            owner = moved[index] >> 3
            owner_y, owner_x = owner >> 2, owner & 3
            found = jnp.where(on_x, owner_y, owner_x) == across
            source = (here - jnp.where(on_x, owner_x, owner_y)) & 3
            table[2 * t + s] = jnp.where(found, source * 4 + rank[index], -1)
    for copy in copies:
        copy.wait()


def stage(after, moved_blocks, values):
    n = len(values)
    table, *staged = pl.pallas_call(
        stage_kernel,
        out_shape=[jax.ShapeDtypeStruct((2 * SIDE,), jnp.int32)]
        + [jax.ShapeDtypeStruct(value.shape, value.dtype) for value in values],
        in_specs=[pl.BlockSpec(memory_space=pl.ANY)] + [HBM] * (1 + n),
        out_specs=[SMEM] + [VMEM] * n,
        scratch_shapes=[
            pltpu.SMEM((MOVED,), jnp.int32),
            pltpu.SMEM((SIDE * SIDE,), jnp.int32),
            pltpu.SMEM((MOVED,), jnp.int32),
            pltpu.SemaphoreType.DMA((n + 1,)),
        ],
        compiler_params=limit(6),
        name="stage",
    )(after, *[in_hbm(value) for value in (moved_blocks, *values)])
    return table, staged


def route_kernel(table, a0, a1, a2, a3, o0, o1, o2, o3):
    arrivals = (a0, a1, a2, a3)
    for t, out in enumerate((o0, o1, o2, o3)):
        for s in range(2):
            entry = table[2 * t + s]
            slot = jnp.maximum(entry, 0) & 3
            value = jnp.zeros(out.shape[1:], out.dtype)
            for k in range(SIDE):
                value = jnp.where((entry >> 2) == k, arrivals[k][slot], value)
            out[s] = value


def route(table, arrivals):
    _, share, rows = arrivals[0].shape
    return pl.pallas_call(
        route_kernel,
        out_shape=[jax.ShapeDtypeStruct((2, share, rows), jnp.bfloat16)] * SIDE,
        in_specs=[SMEM] + [VMEM] * SIDE,
        out_specs=[VMEM] * SIDE,
        compiler_params=limit(6),
        name="route",
    )(table, *arrivals)


def radiate_kernel(a0, a1, a2, a3, geometry, columns, keep, give):
    core = lax.axis_index("row")
    partial = []
    for s in range(2):
        panel = (a0[s] + a1[s]) + (a2[s] + a3[s])
        columns[s] = panel
        partial.append(jnp.dot(panel, geometry[s], preferred_element_type=jnp.float32))
    keep[...] = jnp.where(core == 0, partial[0], partial[1])
    give[...] = jnp.where(core == 0, partial[1], partial[0])


def radiate(arrivals, geometry):
    _, share, rows = arrivals[0].shape
    half = jax.ShapeDtypeStruct((share, geometry.shape[2]), jnp.float32)
    return pl.pallas_call(
        radiate_kernel,
        out_shape=[jax.ShapeDtypeStruct((2, share, rows), jnp.bfloat16), half, half],
        in_specs=[VMEM] * 5,
        out_specs=[VMEM] * 3,
        compiler_params=limit(8),
        name="radiate",
    )(*arrivals, geometry)


def first_row(shift, share):
    part = (lax.axis_index("exc") - shift) & (SLICES - 1)
    return pl.multiple_of(part * share, share)


def assemble_kernel(own, up, down, far, out):
    share = own.shape[0]
    for shift, value in ((0, own), (1, up), (-1, down), (2, far)):
        out[pl.ds(first_row(shift, share), share), :] = value[...]


def assemble(pieces):
    share, width = pieces[0].shape
    return pl.pallas_call(
        assemble_kernel,
        out_shape=jax.ShapeDtypeStruct((SLICES * share, width), jnp.bfloat16),
        in_specs=[VMEM] * 4,
        out_specs=VMEM,
        compiler_params=limit(4),
        name="assemble",
    )(*pieces)


def weigh_kernel(partners, trans, patt, after, out):
    columns = trans.shape[1]
    rows = patt.shape[1]

    def body(i, carry):
        for j in range(columns):
            pattern = patt[partners[j, i] & 7].astype(jnp.float32)
            out[i, j * rows : (j + 1) * rows, :] = (pattern * trans[i, j : j + 1, :]).astype(jnp.bfloat16)
        return carry

    lax.fori_loop(0, trans.shape[0], body, 0)


def weigh(partners, translation, patterns, after):
    moved, columns, width = translation.shape
    return pl.pallas_call(
        weigh_kernel,
        out_shape=pltpu.VMEM((moved, columns * patterns.shape[1], width), jnp.bfloat16),
        in_specs=[SMEM, VMEM, VMEM, pl.BlockSpec(memory_space=pl.ANY)],
        out_specs=VMEM,
        compiler_params=limit(4),
        name="weigh",
    )(partners, translation, patterns, after)


def couple(pieces, weighted, columns, so_far=None, addends=None):
    n = len(pieces)
    moved, tall, width = weighted.shape
    rows = tall // columns
    basis = pieces[0][2].shape[1]
    together = 4

    def kernel(weights, *refs):
        piece_refs = refs[:n]
        copies = []
        if addends is None:
            out, buf, sem = refs[-3:]
        else:
            left, right = refs[n : n + 2]
            out, total_out, buf, sem, total, total_sem = refs[-6:]
            total[...] = left[...] + right[...]
            copies.append(pltpu.make_async_copy(total, total_out, total_sem))
            copies[0].start()
        me = lax.axis_index("blk")
        core = lax.axis_index("row")
        y, x = me >> 2, me & 3
        for p, (leg, own, _) in enumerate(pieces):
            holder = core if own else 1 - core
            near = jnp.where(holder == 0, x, y)
            across = (jnp.where(holder == 0, y, x) - leg) & 3
            ids = []
            for k in range(SIDE):
                first = (near - k) & 3
                block = jnp.where(holder == 0, across * SIDE + first, first * SIDE + across)
                ids.append(2 * block + holder)
            halves = 2 if p == n - 1 else 1
            for part in range(halves):
                some = range(part * SIDE // halves, (part + 1) * SIDE // halves)
                rads = {k: piece_refs[p][k].T for k in some}
                for first in range(0, columns, together):
                    for k in some:
                        some_rows = weights[ids[k], first * rows : (first + together) * rows, :]
                        block = jnp.dot(some_rows, rads[k], preferred_element_type=jnp.float32)
                        buf[p, k, first : first + together] = block.astype(jnp.bfloat16).reshape(together, rows, basis)
                for k in some:
                    copy = pltpu.make_async_copy(buf.at[p, k], out.at[ids[k]], sem.at[p, k])
                    copy.start()
                    copies.append(copy)
        for copy in copies:
            copy.wait()

    operands = [weighted, *[piece[2] for piece in pieces], *(addends or ())]
    in_specs = [VMEM] * len(operands)
    aliases = {}
    if so_far is not None:
        in_specs.append(pl.BlockSpec(memory_space=pl.ANY))
        aliases = {len(operands): 0}
        operands.append(so_far)
    shapes = [jax.ShapeDtypeStruct((moved, columns, rows, basis), jnp.bfloat16)]
    scratch = [pltpu.VMEM((n, SIDE, columns, rows, basis), jnp.bfloat16), pltpu.SemaphoreType.DMA((n, SIDE))]
    if addends is not None:
        shapes.append(jax.ShapeDtypeStruct(addends[0].shape, addends[0].dtype))
        scratch += [pltpu.VMEM(addends[0].shape, addends[0].dtype), pltpu.SemaphoreType.DMA]
    results = pl.pallas_call(
        kernel,
        out_shape=shapes,
        in_specs=in_specs,
        out_specs=[pl.BlockSpec(memory_space=pl.ANY)] * len(shapes),
        scratch_shapes=scratch,
        input_output_aliases=aliases,
        compiler_params=limit(8),
        cost_estimate=pl.CostEstimate(
            flops=2 * n * SIDE * tall * width * basis,
            bytes_accessed=n * SIDE * tall * basis * 2,
            transcendentals=0,
        ),
        name="couple",
    )(*operands)
    return results[0] if addends is None else results


def hold_kernel(value, after, out):
    pass


def hold(value, after):
    return pl.pallas_call(
        hold_kernel,
        out_shape=jax.ShapeDtypeStruct(value.shape, value.dtype),
        in_specs=[pl.BlockSpec(memory_space=pl.ANY)] * 2,
        out_specs=pl.BlockSpec(memory_space=pl.ANY),
        input_output_aliases={0: 0},
        compiler_params=limit(1),
        name="hold",
    )(value, after)


def project_kernel(excitations, own, up, down, far, out, panel):
    share = own.shape[1]
    for shift, value in ((0, own), (1, up), (-1, down), (2, far)):
        panel[:, pl.ds(first_row(shift, share), share), :] = value[...]
    for s in range(2):
        out[s] = lax.dot_general(excitations[s], panel[s], NT, preferred_element_type=jnp.float32)


def project(excitations, pieces):
    moved, count, rows = excitations.shape
    basis = SLICES * pieces[0].shape[1]
    return pl.pallas_call(
        project_kernel,
        out_shape=jax.ShapeDtypeStruct((moved, count, basis), jnp.float32),
        in_specs=[VMEM] * 5,
        out_specs=VMEM,
        scratch_shapes=[pltpu.VMEM((2, basis, rows), jnp.bfloat16)],
        compiler_params=limit(6),
        name="project",
    )(excitations, *pieces)


def on_device(panels, patterns, geometry, excitations, moved_blocks, partners, translation):
    outgoing = pick(moved_blocks, panels)
    arrivals = plane_send(outgoing, True)
    table, (geometry, translation, patterns, excitations, partners) = stage(
        outgoing, moved_blocks, [geometry, translation, patterns, excitations, partners.T]
    )
    table, *arrivals = lax.optimization_barrier((table, *arrivals))
    routed = route(table, [outgoing, *arrivals])
    landed = [lax.ppermute(routed[s], AXES, plane_perm(s, False)) for s in range(1, SIDE)]
    weighted = weigh(partners, translation, patterns, routed[0])
    weighted, *landed = lax.optimization_barrier((weighted, *landed))
    columns, keep, give = radiate([routed[0], *landed], geometry)
    radiation = (keep + core_swap(give)).astype(jnp.bfloat16)
    mine = assemble([radiation, *[depth_send(radiation, s) for s in (1, -1, 2)]])

    seen = plane_send(mine, True)
    columns = hold(columns, mine)
    columns_far = depth_send(columns, 2)
    stack = jnp.stack([mine, *seen])
    arrived = plane_send(stack, False)
    columns_up, columns_down = depth_send(columns, 1), depth_send(columns, -1)
    columns_far, stack = lax.optimization_barrier((columns_far, stack))
    depth = weighted, translation.shape[1]
    couplings = couple([(0, True, stack)], *depth)
    couplings, stack, columns_up, columns_down, *arrived = lax.optimization_barrier(
        (couplings, stack, columns_up, columns_down, *arrived)
    )
    other = [(leg, False, core_swap(value)) for leg, value in enumerate([stack, *arrived])]
    projected = project(excitations, [columns, columns_up, columns_down, columns_far])
    came = core_swap(projected)
    couplings = couple([(leg, True, arrived[leg - 1]) for leg in range(1, SIDE)], *depth, couplings)
    couplings, projected = couple(other, *depth, couplings, (projected, came))
    return (couplings, projected)


def solution(mesh):
    placed = (
        P("blk", "row", None),
        P("blk", "row", None),
        P("blk", "row", None),
        P("blk", "exc", "row"),
        P(),
        P(None, ("blk", "exc")),
        P(None, ("blk", "exc"), None),
    )
    return jax.shard_map(
        on_device,
        mesh=mesh,
        in_specs=placed,
        out_specs=(P(None, ("blk", "exc"), "row", None), P("blk", "exc", None)),
        check_vma=False,
    )
```

```python
import jax
import jax.numpy as jnp
from jax import lax
from jax.experimental import pallas as pl
from jax.experimental.pallas import tpu as pltpu
from jax.sharding import PartitionSpec as P

CAP = 3
SIDE = 4
DEPTH = 8
MOVED = 32
SLICES = 4
ORDER = (1, 3, 2)
MIB = 2**20
AXES = ("blk", "exc", "row")
NT = (((1,), (1,)), ((), ()))
SMEM = pl.BlockSpec(memory_space=pltpu.SMEM)
VMEM = pl.BlockSpec(memory_space=pltpu.VMEM)
HBM = pl.BlockSpec(memory_space=pltpu.HBM)


def device_id(y, x, z, core):
    return ((y * SIDE + x) * DEPTH + z) * 2 + core


def plane_perm(shift, first):
    pairs = []
    for y in range(SIDE):
        for x in range(SIDE):
            for z in range(DEPTH):
                for core in range(2):
                    along_x = (core == 0) == first
                    y_to = y if along_x else (y + shift) % SIDE
                    x_to = (x + shift) % SIDE if along_x else x
                    pairs.append((device_id(y, x, z, core), device_id(y_to, x_to, z, core)))
    return pairs


def depth_perm(shift):
    pairs = []
    for y in range(SIDE):
        for x in range(SIDE):
            for z in range(DEPTH):
                for core in range(2):
                    step = -shift if core and shift == 2 else shift
                    pairs.append((device_id(y, x, z, core), device_id(y, x, (z + step) % DEPTH, core)))
    return pairs


def plane_send(value, first):
    sent = {s: lax.ppermute(value, AXES, plane_perm(s, first)) for s in ORDER}
    return [sent[s] for s in range(1, SIDE)]


def depth_send(value, shift):
    return lax.ppermute(value, AXES, depth_perm(shift))


def core_swap(value):
    return lax.ppermute(value, "row", [(0, 1), (1, 0)])


def limit(mib):
    return pltpu.CompilerParams(vmem_limit_bytes=mib * MIB)


def pick_kernel(moved_hbm, panels, out, moved, buf, sem):
    index_copy = pltpu.make_async_copy(moved_hbm, moved, sem.at[CAP])
    index_copy.start()
    me = lax.axis_index("blk")
    part = lax.axis_index("exc") & (SLICES - 1)
    slots = [jnp.int32(0)] * CAP
    count = jnp.int32(0)
    index_copy.wait()
    for i in range(MOVED):
        block = moved[i]
        mine = (block >> 3) == me
        slots = [jnp.where(mine & (count == s), block & 7, slots[s]) for s in range(CAP)]
        count = count + mine.astype(jnp.int32)
    copies = []
    for s in range(CAP):
        copy = pltpu.make_async_copy(panels.at[slots[s]], buf.at[s], sem.at[s])
        copy.start()
        copies.append(copy)
    width = buf.shape[2]
    share = out.shape[1]
    rows = lax.broadcasted_iota(jnp.int32, (share, width), 0)
    cols = lax.broadcasted_iota(jnp.int32, (share, width), 1)
    chosen = jnp.where(cols == rows + part * share, 1.0, 0.0).astype(jnp.bfloat16)
    for s in range(CAP):
        copies[s].wait()
        out[s] = lax.dot_general(chosen, buf[s], NT, preferred_element_type=jnp.float32).astype(jnp.bfloat16)


def in_hbm(value):
    return pltpu.with_memory_space_constraint(value, pltpu.HBM)


def pick(moved_blocks, panels):
    blocks, rows, width = panels.shape
    return pl.pallas_call(
        pick_kernel,
        out_shape=jax.ShapeDtypeStruct((CAP, width // SLICES, rows), jnp.bfloat16),
        in_specs=[HBM] * 2,
        out_specs=VMEM,
        scratch_shapes=[
            pltpu.SMEM((MOVED,), jnp.int32),
            pltpu.VMEM((CAP, rows, width), jnp.bfloat16),
            pltpu.SemaphoreType.DMA((CAP + 1,)),
        ],
        compiler_params=limit(6),
        name="pick",
    )(in_hbm(moved_blocks), in_hbm(panels))


def stage_kernel(after, moved_hbm, *refs):
    n = (len(refs) - 5) // 2
    table = refs[n]
    moved, count, rank, sem = refs[-4:]
    copies = [pltpu.make_async_copy(refs[k], refs[n + 1 + k], sem.at[k]) for k in range(n)]
    index_copy = pltpu.make_async_copy(moved_hbm, moved, sem.at[n])
    index_copy.start()
    for copy in copies:
        copy.start()
    me = lax.axis_index("blk")
    core = lax.axis_index("row")
    y, x = me >> 2, me & 3
    on_x = core == 0
    here = jnp.where(on_x, x, y)
    across = jnp.where(on_x, y, x)
    for g in range(SIDE * SIDE):
        count[g] = 0
    index_copy.wait()
    for i in range(MOVED):
        owner = moved[i] >> 3
        seen = count[owner]
        rank[i] = seen
        count[owner] = seen + 1
    for t in range(SIDE):
        target = (across + t) & 3
        block = jnp.where(on_x, target * SIDE + here, here * SIDE + target)
        for s in range(2):
            index = 2 * block + s
            owner = moved[index] >> 3
            owner_y, owner_x = owner >> 2, owner & 3
            found = jnp.where(on_x, owner_y, owner_x) == across
            source = (here - jnp.where(on_x, owner_x, owner_y)) & 3
            table[2 * t + s] = jnp.where(found, source * 4 + rank[index], -1)
    for copy in copies:
        copy.wait()


def stage(after, moved_blocks, values):
    n = len(values)
    table, *staged = pl.pallas_call(
        stage_kernel,
        out_shape=[jax.ShapeDtypeStruct((2 * SIDE,), jnp.int32)]
        + [jax.ShapeDtypeStruct(value.shape, value.dtype) for value in values],
        in_specs=[pl.BlockSpec(memory_space=pl.ANY)] + [HBM] * (1 + n),
        out_specs=[SMEM] + [VMEM] * n,
        scratch_shapes=[
            pltpu.SMEM((MOVED,), jnp.int32),
            pltpu.SMEM((SIDE * SIDE,), jnp.int32),
            pltpu.SMEM((MOVED,), jnp.int32),
            pltpu.SemaphoreType.DMA((n + 1,)),
        ],
        compiler_params=limit(6),
        name="stage",
    )(after, *[in_hbm(value) for value in (moved_blocks, *values)])
    return table, staged


def route_kernel(table, a0, a1, a2, a3, o0, o1, o2, o3):
    arrivals = (a0, a1, a2, a3)
    for t, out in enumerate((o0, o1, o2, o3)):
        for s in range(2):
            entry = table[2 * t + s]
            slot = jnp.maximum(entry, 0) & 3
            value = jnp.zeros(out.shape[1:], out.dtype)
            for k in range(SIDE):
                value = jnp.where((entry >> 2) == k, arrivals[k][slot], value)
            out[s] = value


def route(table, arrivals):
    _, share, rows = arrivals[0].shape
    return pl.pallas_call(
        route_kernel,
        out_shape=[jax.ShapeDtypeStruct((2, share, rows), jnp.bfloat16)] * SIDE,
        in_specs=[SMEM] + [VMEM] * SIDE,
        out_specs=[VMEM] * SIDE,
        compiler_params=limit(6),
        name="route",
    )(table, *arrivals)


def radiate_kernel(a0, a1, a2, a3, geometry, columns, keep, give):
    core = lax.axis_index("row")
    partial = []
    for s in range(2):
        panel = (a0[s] + a1[s]) + (a2[s] + a3[s])
        columns[s] = panel
        partial.append(jnp.dot(panel, geometry[s], preferred_element_type=jnp.float32))
    keep[...] = jnp.where(core == 0, partial[0], partial[1])
    give[...] = jnp.where(core == 0, partial[1], partial[0])


def radiate(arrivals, geometry):
    _, share, rows = arrivals[0].shape
    half = jax.ShapeDtypeStruct((share, geometry.shape[2]), jnp.float32)
    return pl.pallas_call(
        radiate_kernel,
        out_shape=[jax.ShapeDtypeStruct((2, share, rows), jnp.bfloat16), half, half],
        in_specs=[VMEM] * 5,
        out_specs=[VMEM] * 3,
        compiler_params=limit(8),
        name="radiate",
    )(*arrivals, geometry)


def first_row(shift, share):
    part = (lax.axis_index("exc") - shift) & (SLICES - 1)
    return pl.multiple_of(part * share, share)


def assemble_kernel(own, up, down, far, out):
    share = own.shape[0]
    for shift, value in ((0, own), (1, up), (-1, down), (2, far)):
        out[pl.ds(first_row(shift, share), share), :] = value[...]


def assemble(pieces):
    share, width = pieces[0].shape
    return pl.pallas_call(
        assemble_kernel,
        out_shape=jax.ShapeDtypeStruct((SLICES * share, width), jnp.bfloat16),
        in_specs=[VMEM] * 4,
        out_specs=VMEM,
        compiler_params=limit(4),
        name="assemble",
    )(*pieces)


def weigh_kernel(partners, trans, patt, after, out):
    columns = trans.shape[1]
    rows = patt.shape[1]

    def body(i, carry):
        for j in range(columns):
            pattern = patt[partners[j, i] & 7].astype(jnp.float32)
            out[i, j * rows : (j + 1) * rows, :] = (pattern * trans[i, j : j + 1, :]).astype(jnp.bfloat16)
        return carry

    lax.fori_loop(0, trans.shape[0], body, 0)


def weigh(partners, translation, patterns, after):
    moved, columns, width = translation.shape
    return pl.pallas_call(
        weigh_kernel,
        out_shape=pltpu.VMEM((moved, columns * patterns.shape[1], width), jnp.bfloat16),
        in_specs=[SMEM, VMEM, VMEM, pl.BlockSpec(memory_space=pl.ANY)],
        out_specs=VMEM,
        compiler_params=limit(4),
        name="weigh",
    )(partners, translation, patterns, after)


def couple(pieces, weighted, columns, so_far=None, addends=None):
    n = len(pieces)
    moved, tall, width = weighted.shape
    rows = tall // columns
    basis = pieces[0][2].shape[1]
    together = 4

    def kernel(weights, *refs):
        piece_refs = refs[:n]
        copies = []
        if addends is None:
            out, buf, sem = refs[-3:]
        else:
            left, right = refs[n : n + 2]
            out, total_out, buf, sem, total, total_sem = refs[-6:]
            total[...] = left[...] + right[...]
            copies.append(pltpu.make_async_copy(total, total_out, total_sem))
            copies[0].start()
        me = lax.axis_index("blk")
        core = lax.axis_index("row")
        y, x = me >> 2, me & 3
        for p, (leg, own, _) in enumerate(pieces):
            holder = core if own else 1 - core
            near = jnp.where(holder == 0, x, y)
            across = (jnp.where(holder == 0, y, x) - leg) & 3
            ids = []
            for k in range(SIDE):
                first = (near - k) & 3
                block = jnp.where(holder == 0, across * SIDE + first, first * SIDE + across)
                ids.append(2 * block + holder)
            halves = 2 if p == n - 1 else 1
            for part in range(halves):
                some = range(part * SIDE // halves, (part + 1) * SIDE // halves)
                rads = {k: piece_refs[p][k].T for k in some}
                for first in range(0, columns, together):
                    for k in some:
                        some_rows = weights[ids[k], first * rows : (first + together) * rows, :]
                        block = jnp.dot(some_rows, rads[k], preferred_element_type=jnp.float32)
                        buf[p, k, first : first + together] = block.astype(jnp.bfloat16).reshape(together, rows, basis)
                for k in some:
                    copy = pltpu.make_async_copy(buf.at[p, k], out.at[ids[k]], sem.at[p, k])
                    copy.start()
                    copies.append(copy)
        for copy in copies:
            copy.wait()

    operands = [weighted, *[piece[2] for piece in pieces], *(addends or ())]
    in_specs = [VMEM] * len(operands)
    aliases = {}
    if so_far is not None:
        in_specs.append(pl.BlockSpec(memory_space=pl.ANY))
        aliases = {len(operands): 0}
        operands.append(so_far)
    shapes = [jax.ShapeDtypeStruct((moved, columns, rows, basis), jnp.bfloat16)]
    scratch = [pltpu.VMEM((n, SIDE, columns, rows, basis), jnp.bfloat16), pltpu.SemaphoreType.DMA((n, SIDE))]
    if addends is not None:
        shapes.append(jax.ShapeDtypeStruct(addends[0].shape, addends[0].dtype))
        scratch += [pltpu.VMEM(addends[0].shape, addends[0].dtype), pltpu.SemaphoreType.DMA]
    results = pl.pallas_call(
        kernel,
        out_shape=shapes,
        in_specs=in_specs,
        out_specs=[pl.BlockSpec(memory_space=pl.ANY)] * len(shapes),
        scratch_shapes=scratch,
        input_output_aliases=aliases,
        compiler_params=limit(8),
        cost_estimate=pl.CostEstimate(
            flops=2 * n * SIDE * tall * width * basis,
            bytes_accessed=n * SIDE * tall * basis * 2,
            transcendentals=0,
        ),
        name="couple",
    )(*operands)
    return results[0] if addends is None else results


def hold_kernel(value, after, out):
    pass


def hold(value, after):
    return pl.pallas_call(
        hold_kernel,
        out_shape=jax.ShapeDtypeStruct(value.shape, value.dtype),
        in_specs=[pl.BlockSpec(memory_space=pl.ANY)] * 2,
        out_specs=pl.BlockSpec(memory_space=pl.ANY),
        input_output_aliases={0: 0},
        compiler_params=limit(1),
        name="hold",
    )(value, after)


def project_kernel(excitations, own, up, down, far, out, panel):
    share = own.shape[1]
    for shift, value in ((0, own), (1, up), (-1, down), (2, far)):
        panel[:, pl.ds(first_row(shift, share), share), :] = value[...]
    for s in range(2):
        out[s] = lax.dot_general(excitations[s], panel[s], NT, preferred_element_type=jnp.float32)


def project(excitations, pieces):
    moved, count, rows = excitations.shape
    basis = SLICES * pieces[0].shape[1]
    return pl.pallas_call(
        project_kernel,
        out_shape=jax.ShapeDtypeStruct((moved, count, basis), jnp.float32),
        in_specs=[VMEM] * 5,
        out_specs=VMEM,
        scratch_shapes=[pltpu.VMEM((2, basis, rows), jnp.bfloat16)],
        compiler_params=limit(6),
        name="project",
    )(excitations, *pieces)


def on_device(panels, patterns, geometry, excitations, moved_blocks, partners, translation):
    outgoing = pick(moved_blocks, panels)
    arrivals = plane_send(outgoing, True)
    table, (geometry, translation, patterns, excitations, partners) = stage(
        outgoing, moved_blocks, [geometry, translation, patterns, excitations, partners.T]
    )
    table, *arrivals = lax.optimization_barrier((table, *arrivals))
    routed = route(table, [outgoing, *arrivals])
    landed = [lax.ppermute(routed[s], AXES, plane_perm(s, False)) for s in range(1, SIDE)]
    weighted = weigh(partners, translation, patterns, routed[0])
    weighted, *landed = lax.optimization_barrier((weighted, *landed))
    columns, keep, give = radiate([routed[0], *landed], geometry)
    radiation = (keep + core_swap(give)).astype(jnp.bfloat16)
    mine = assemble([radiation, *[depth_send(radiation, s) for s in (1, -1, 2)]])

    seen = plane_send(mine, True)
    columns = hold(columns, mine)
    columns_far = depth_send(columns, 2)
    stack = jnp.stack([mine, *seen])
    arrived = plane_send(stack, False)
    columns_up, columns_down = depth_send(columns, 1), depth_send(columns, -1)
    columns_far, stack = lax.optimization_barrier((columns_far, stack))
    depth = weighted, translation.shape[1]
    couplings = couple([(0, True, stack)], *depth)
    couplings, columns_up, columns_down = lax.optimization_barrier((couplings, columns_up, columns_down))
    projected = project(excitations, [columns, columns_up, columns_down, columns_far])
    couplings, projected, stack, *arrived = lax.optimization_barrier((couplings, projected, stack, *arrived))
    other = [(leg, False, core_swap(value)) for leg, value in enumerate([stack, *arrived])]
    came = core_swap(projected)
    couplings = couple([(leg, True, arrived[leg - 1]) for leg in range(1, SIDE)], *depth, couplings)
    couplings, projected = couple(other, *depth, couplings, (projected, came))
    return (couplings, projected)


def solution(mesh):
    placed = (
        P("blk", "row", None),
        P("blk", "row", None),
        P("blk", "row", None),
        P("blk", "exc", "row"),
        P(),
        P(None, ("blk", "exc")),
        P(None, ("blk", "exc"), None),
    )
    return jax.shard_map(
        on_device,
        mesh=mesh,
        in_specs=placed,
        out_specs=(P(None, ("blk", "exc"), "row", None), P("blk", "exc", None)),
        check_vma=False,
    )
```
